128 devices in a mesh: row: 8 (over x, core), col: 16 (over y, z).
Axes of the slice: x: 4, y: 4, z: 4, core: 2. Of those that a mesh axis runs over, the one named last changes fastest.
Arguments:
- object_slices: float32 [2, 2, 2048, 4096], P(None, None, 'row', 'col'), may hold values from -5 to 5
- probe: float32 [2, 128, 128], replicated, may hold values from -6 to 6
- amplitudes: float32 [8, 16, 16, 128, 128], P('row', 'col'), may hold values from 0.3 to 3
- scan_pos: int32 [2, 8, 16, 16], P(None, 'row', 'col'), may hold values from 0 to 4095, as said below
- scan_count: int32 [8, 16], P('row', 'col'), may hold values from 0 to 16, as said below
Outputs:
- object_new: float32 [2, 2, 2048, 4096], P(None, None, 'row', 'col')
The draws below stay inside these ranges and needn't reach their ends.
Inputs may be any that keep to these rules, and one draw needn't show every extreme that they name: `scan_pos`: entry [0, i, j, k] is the pixel row and [1, i, j, k] the pixel column of the centre of slot k of tile (i, j); the centre lies within that tile's 256 x 256 pixels, also for slots that are not live. The live scans of a tile are its first scan_count slots; in every tile row the counts of its 16 tiles sum to exactly 128, and some tile of every row holds 16 scans.
All inputs are finite; a program needn't handle non-finite values.
Results may differ from the reference program's by a relative error of at most 0.00029.
Values sent between devices are 32-bit elements; how exact they have to be, the bound alone decides.
A program may use at most 128 MiB of HBM per device.

```python
import math
import jax
import jax.numpy as jnp
from jax import lax

P_SIZE = 128
SLICES = 2
ITERS = 2
TR = 256
TC = 256
OWN_CAP = 16
GRID_R = 8
GRID_C = 16
NR = 2048
NC = 4096


def draw_scan_count(key, part):

    def one_row(row_key):
        key_order, key_first = jax.random.split(row_key)
        column_order = jax.random.permutation(key_order, GRID_C)
        first_half = jax.random.randint(key_first, (GRID_C // 2,), 0, OWN_CAP + 1)
        first_half = first_half.at[0].set(OWN_CAP)
        paired = jnp.stack([first_half, OWN_CAP - first_half], axis=1).reshape(GRID_C)
        return jnp.zeros((GRID_C,), jnp.int32).at[column_order].set(paired.astype(jnp.int32))
    return jax.vmap(one_row)(jax.random.split(jax.random.fold_in(key, 11), GRID_R))


def draw_scan_pos(key, part):
    key_rows, key_cols = jax.random.split(jax.random.fold_in(key, 23))
    offset_rows = jax.random.randint(key_rows, (GRID_R, GRID_C, OWN_CAP), 0, TR)
    offset_cols = jax.random.randint(key_cols, (GRID_R, GRID_C, OWN_CAP), 0, TC)
    offset_rows = offset_rows.at[GRID_R - 1, GRID_C - 1, 0].set(TR - 1).at[0, 0, 1].set(0)
    offset_cols = offset_cols.at[GRID_R - 1, GRID_C - 1, 0].set(TC - 1).at[0, 0, 1].set(0)
    start_rows = (jnp.arange(GRID_R, dtype=jnp.int32) * TR)[:, None, None]
    start_cols = (jnp.arange(GRID_C, dtype=jnp.int32) * TC)[None, :, None]
    return jnp.stack([offset_rows + start_rows, offset_cols + start_cols]).astype(jnp.int32)


def block_scale(stream_key, shape, shards, smallest, high):
    factor_of, own = 1.0, jax.random.fold_in(stream_key, 6)
    for dim, shards_of in shards:
        steps = jnp.exp(jax.random.uniform(jax.random.fold_in(own, dim), (shards_of,), jnp.float32, smallest / len(shards), high / len(shards)))
        factor_of = factor_of * jnp.repeat(steps, shape[dim] // shards_of).reshape([-1 if axis == dim else 1 for axis in range(len(shape))])
    return factor_of


def centred(rng, extent, width, most, pieces=(), kind=jnp.bfloat16):
    drawn = width * jax.random.normal(rng, extent, jnp.float32)
    if pieces:
        drawn = drawn * block_scale(rng, extent, pieces, -0.22, 0.18)
    return jnp.clip(drawn, -most, most).astype(kind)


def setup_inputs(seed: int = 0) -> dict:
    keys = jax.random.split(jax.random.key(seed), 6)
    object_slices = centred(keys[0], (SLICES, 2, NR, NC), 0.7, 5.0, ((2, 8), (3, 16)), jnp.float32)
    probe = centred(keys[1], (2, P_SIZE, P_SIZE), 1.0, 6.0, (), jnp.float32)
    amplitudes = jnp.clip(jnp.exp(math.log(3.0) - 2.3025851 * jax.random.uniform(keys[2], (GRID_R, GRID_C, OWN_CAP, P_SIZE, P_SIZE), jnp.float32) ** block_scale(keys[2], (GRID_R, GRID_C, OWN_CAP, P_SIZE, P_SIZE), ((0, 8), (1, 16)), -0.2, 0.2)), 0.3, 3.0)
    scan_pos = draw_scan_pos(jax.random.fold_in(keys[5], 71), 0)
    scan_count = draw_scan_count(jax.random.fold_in(keys[5], 71), 0)
    return {"object_slices": object_slices, "probe": probe, "amplitudes": amplitudes, "scan_pos": scan_pos, "scan_count": scan_count}


modulus_offset = 0.5
fresnel_scale = 0.9

def propagator(frame_size, dtype):
    positions = jnp.arange(frame_size, dtype=jnp.int32)
    frequency = jnp.where(positions < frame_size // 2, positions, positions - frame_size).astype(dtype)
    phase = math.pi * fresnel_scale * (frequency[:, None] ** 2 + frequency[None, :] ** 2) / frame_size
    return jnp.cos(phase) + 1j * jnp.sin(phase)

def slot_gradients(patches, local_amps, probe_c, prop):
    layers = patches.shape[1]
    objects = [patches[:, layer_id, 0] + 1j * patches[:, layer_id, 1] for layer_id in range(layers)]
    incident = [jnp.broadcast_to(probe_c, objects[0].shape)]
    for layer_id in range(layers - 1):
        exit_wave = incident[layer_id] * objects[layer_id]
        spectrum = jnp.fft.fft2(exit_wave, norm='ortho')
        incident.append(jnp.fft.ifft2(prop * spectrum, norm='ortho'))
    psi = jnp.fft.fft2(incident[-1] * objects[-1], norm='ortho')
    modulus = jnp.sqrt(jnp.real(psi) ** 2 + jnp.imag(psi) ** 2 + modulus_offset)
    residual = psi * (1.0 - local_amps / modulus)
    back_wave = jnp.fft.ifft2(residual, norm='ortho')
    gradients = [None] * layers
    for layer_id in reversed(range(layers)):
        grad_c = jnp.conj(incident[layer_id]) * back_wave
        gradients[layer_id] = jnp.stack([jnp.real(grad_c), jnp.imag(grad_c)], axis=1)
        if layer_id > 0:
            adjoint = jnp.conj(objects[layer_id]) * back_wave
            spectrum = jnp.fft.fft2(adjoint, norm='ortho')
            back_wave = jnp.fft.ifft2(jnp.conj(prop) * spectrum, norm='ortho')
    return jnp.stack(gradients, axis=1)

def reference(object_slices, probe, amplitudes, scan_pos, scan_count):
    frame_size = probe.shape[-1]
    half_frame = frame_size // 2
    probe_c = probe[0] + 1j * probe[1]
    prop = propagator(frame_size, probe.dtype)
    tiles = GRID_R * GRID_C
    centre_rows = scan_pos[0].reshape(tiles, OWN_CAP).astype(jnp.int32)
    centre_cols = scan_pos[1].reshape(tiles, OWN_CAP).astype(jnp.int32)
    amps_all = amplitudes.reshape(tiles, OWN_CAP, frame_size, frame_size)
    counts = scan_count.reshape(tiles).astype(jnp.int32)
    slot_ids = jnp.arange(OWN_CAP, dtype=jnp.int32)
    zero_index = jnp.zeros((), jnp.int32)
    current = object_slices
    for iteration in range(ITERS):
        padded = jnp.pad(current, ((0, 0), (0, 0), (half_frame, half_frame), (half_frame, half_frame)))

        def tile_step(tile_id, accumulator):
            rows_here = centre_rows[tile_id]
            cols_here = centre_cols[tile_id]
            patches = jax.vmap(lambda row_at, col_at: lax.dynamic_slice(padded, (zero_index, zero_index, row_at, col_at), (SLICES, 2, frame_size, frame_size)))(rows_here, cols_here)
            live_mask = (slot_ids < counts[tile_id]).astype(padded.dtype)
            gradients = slot_gradients(patches, amps_all[tile_id], probe_c, prop) * live_mask[:, None, None, None, None]

            def add_one(item, inner):
                corner = (zero_index, zero_index, rows_here[item], cols_here[item])
                current_block = lax.dynamic_slice(inner, corner, (SLICES, 2, frame_size, frame_size))
                return lax.dynamic_update_slice(inner, current_block + gradients[item], corner)
            return lax.fori_loop(0, OWN_CAP, add_one, accumulator)
        accumulator = lax.fori_loop(0, tiles, tile_step, jnp.zeros_like(padded))
        current = current - accumulator[:, :, half_frame:half_frame + NR, half_frame:half_frame + NC]
    return current
```

```python
import functools
import math

import jax
import jax.numpy as jnp
import numpy as np
from jax import lax
from jax.experimental import pallas as pl
from jax.experimental.pallas import tpu as pltpu
from jax.sharding import PartitionSpec as P

ITERS = 2
MESH = pl.DeviceIdType.MESH
F32 = jnp.float32
BF16 = jnp.bfloat16

modulus_offset = 0.5
fresnel_scale = 0.9

N = 128
T = 256
E = T + N
HALF = N // 2
LANES = E // N
SLOTS = 16
GROUP = 4
GROWS = N + 16


def tables():
    positions = np.arange(N)
    frequency = np.where(positions < N // 2, positions, positions - N).astype(np.float64)
    angle = -2.0 * math.pi / N * (np.outer(positions, positions) % N)
    dft = (np.cos(angle) + 1j * np.sin(angle)) / math.sqrt(N)
    phase = math.pi * fresnel_scale * frequency**2 / N
    spread = np.conj(dft) @ (np.exp(1j * phase)[:, None] * dft)
    spread = 0.5 * (spread + spread.T)
    made = []
    for matrix in (spread, dft):
        left = np.block([[matrix.real, -matrix.imag], [matrix.imag, matrix.real]])
        for form in (left, left.T):
            high = form.astype(np.float32).astype(BF16)
            low = (form - high.astype(np.float64)).astype(np.float32).astype(BF16)
            made += [high, low]
    return np.stack(made)


def split(value):
    high = value.astype(BF16)
    return high, (value - high.astype(F32)).astype(BF16)


def dot(a, b):
    return jnp.dot(a, b, preferred_element_type=F32)


def kernel(
    rows_n, cols_n,
    pos_ref, count_ref, obj_ref, probe_ref, amps_ref, tab_ref,
    out_ref,
    ext0, ext1, acc0, acc1, inc_ref, lay_ref, grad_ref,
    halo_src, halo_dst, up_ref, down_ref, left_ref, right_ref,
    fin_up, fin_down, fin_src, fin_dst,
    send_sem, recv_sem,
):
    row, col = lax.axis_index("row"), lax.axis_index("col")
    up = (lax.rem(row + rows_n - 1, rows_n), col)
    down = (lax.rem(row + 1, rows_n), col)
    left = (row, lax.rem(col + cols_n - 1, cols_n))
    right = (row, lax.rem(col + 1, cols_n))
    has_up, has_down = row > 0, row < rows_n - 1
    has_left, has_right = col > 0, col < cols_n - 1
    ext, acc = (ext0, ext1), (acc0, acc1)
    used = [0]

    barrier = pltpu.get_barrier_semaphore()
    for device in (up, down, left, right):
        pl.semaphore_signal(barrier, inc=1, device_id=device, device_id_type=MESH)

    def copy(source, target, device):
        index = used[0]
        used[0] += 1
        made = pltpu.make_async_remote_copy(
            src_ref=source, dst_ref=target, send_sem=send_sem.at[index],
            recv_sem=recv_sem.at[index], device_id=device, device_id_type=MESH,
        )
        made.start()
        return made

    def wait(copies):
        for made in copies:
            made.wait()

    lane = lax.broadcasted_iota(jnp.int32, (N, N), 1)
    low = lane < HALF

    def swap(value):
        return pltpu.roll(value, HALF, 1)

    low_t = lax.broadcasted_iota(jnp.int32, (T, N), 1) < HALF
    for s in range(2):
        first = [obj_ref[s, c, :, 0:N] for c in range(2)]
        last = [obj_ref[s, c, :, N : 2 * N] for c in range(2)]
        halo_src[s, 0] = jnp.where(low_t, first[1], swap(first[0]))
        halo_src[s, 1] = jnp.where(low_t, swap(last[0]), last[1])

    pl.semaphore_wait(barrier, 4)
    side = [
        [copy(halo_src.at[s, 0], halo_dst.at[s, 1], left), copy(halo_src.at[s, 1], halo_dst.at[s, 0], right)]
        for s in range(2)
    ]

    for s in range(2):
        for c in range(2):
            first, last = swap(obj_ref[s, c, :, 0:N]), swap(obj_ref[s, c, :, N : 2 * N])
            ext[s][c, 1, HALF : HALF + T, :] = jnp.where(low_t, first, last)

    def clear(k, carry):
        for c in range(2):
            for t in range(LANES):
                grad_ref[k, c, t, 0:8, :] = jnp.zeros((8, N), F32)
                grad_ref[k, c, t, GROWS - 8 : GROWS, :] = jnp.zeros((8, N), F32)
        return carry

    lax.fori_loop(0, SLOTS, clear, 0)

    edge = []
    for s in range(2):
        wait(side[s])
        from_left = jnp.where(has_left, halo_dst[s, 0], 0.0)
        from_right = jnp.where(has_right, halo_dst[s, 1], 0.0)
        for c in range(2):
            first, last = swap(obj_ref[s, c, :, 0:N]), swap(obj_ref[s, c, :, N : 2 * N])
            ext[s][c, 0, HALF : HALF + T, :] = jnp.where(low_t, from_left if c == 0 else swap(from_left), first)
            ext[s][c, 2, HALF : HALF + T, :] = jnp.where(low_t, last, from_right if c == 0 else swap(from_right))
        edge.append([
            copy(ext[s].at[:, :, HALF : 2 * HALF, :], ext[s].at[:, :, E - HALF : E, :], up),
            copy(ext[s].at[:, :, T : T + HALF, :], ext[s].at[:, :, 0:HALF, :], down),
        ])

    def border(s):
        wait(edge[s])
        ext[s][:, :, 0:HALF, :] = jnp.where(has_up, ext[s][:, :, 0:HALF, :], 0.0)
        ext[s][:, :, E - HALF : E, :] = jnp.where(has_down, ext[s][:, :, E - HALF : E, :], 0.0)

    def place(k):
        at_row, at_col = lax.rem(pos_ref[0, k], T), lax.rem(pos_ref[1, k], T)
        return at_row, at_col // N, at_col % N

    def patch(s, k):
        at_row, at_lane, shift = place(k)
        back = (N - shift) % N
        parts = []
        for c in range(2):
            here = ext[s][c, at_lane, pl.ds(at_row, N), :]
            after = ext[s][c, at_lane + 1, pl.ds(at_row, N), :]
            parts.append(pltpu.roll(jnp.where(lane >= shift, here, after), back, 1))
        return parts

    def put(k, parts):
        at_row, at_lane, shift = place(k)
        live = (k < count_ref[0, 0]).astype(F32)
        second = live * at_lane.astype(F32)
        first = live - second
        for c in range(2):
            moved = pltpu.roll(parts[c], shift, 1)
            here = jnp.where(lane >= shift, moved, 0.0)
            after = jnp.where(lane >= shift, 0.0, moved)
            grad_ref[k, c, 0, 8 : 8 + N, :] = here * first
            grad_ref[k, c, 1, 8 : 8 + N, :] = here * second + after * first
            grad_ref[k, c, 2, 8 : 8 + N, :] = after * second

    def apply(which, waves):
        high_l, low_l = tab_ref[2 * which], tab_ref[2 * which + 1]
        other = which ^ 1
        high_r, low_r = tab_ref[2 * other], tab_ref[2 * other + 1]
        (re_a, im_a), (re_b, im_b) = waves
        value = jnp.concatenate(
            [jnp.concatenate([re_a, re_b], axis=1), jnp.concatenate([im_a, im_b], axis=1)], axis=0
        )
        high, low_part = split(value)
        mid = dot(high_l, high) + dot(high_l, low_part) + dot(low_l, high)
        value = jnp.concatenate(
            [
                jnp.concatenate([mid[:N, :N], mid[N:, :N]], axis=1),
                jnp.concatenate([mid[:N, N:], mid[N:, N:]], axis=1),
            ],
            axis=0,
        )
        high, low_part = split(value)
        done = dot(high, high_r) + dot(low_part, high_r) + dot(high, low_r)
        return (done[:N, :N], done[:N, N:]), (done[N:, :N], done[N:, N:])

    def product(a, b):
        return a[0] * b[0] - a[1] * b[1], a[0] * b[1] + a[1] * b[0]

    def product_conj(a, b):
        return a[0] * b[0] + a[1] * b[1], a[0] * b[1] - a[1] * b[0]

    SPREAD, SPREAD_ADJ, DFT, DFT_INV = 0, 1, 2, 3

    def loop(stage, start, stop):
        def step(g, carry):
            for pair in range(GROUP // 2):
                stage([g * GROUP + 2 * pair, g * GROUP + 2 * pair + 1])
            return carry

        lax.fori_loop(start // GROUP, stop // GROUP, step, 0)

    def ahead(slots):
        illum = (probe_ref[0], probe_ref[1])
        waves = apply(SPREAD, [product(illum, patch(0, k)) for k in slots])
        for k, wave in zip(slots, waves):
            inc_ref[k, 0], inc_ref[k, 1] = wave

    def detect(slots):
        exits = []
        for k in slots:
            layer = patch(1, k)
            lay_ref[k, 0], lay_ref[k, 1] = layer
            exits.append(product((inc_ref[k, 0], inc_ref[k, 1]), layer))
        residuals = []
        for k, (re, im) in zip(slots, apply(DFT, exits)):
            factor = 1.0 - amps_ref[k] / jnp.sqrt(re * re + im * im + modulus_offset)
            residuals.append((re * factor, im * factor))
        for k, back in zip(slots, apply(DFT_INV, residuals)):
            put(k, product_conj((inc_ref[k, 0], inc_ref[k, 1]), back))
            lay_ref[k, 0], lay_ref[k, 1] = product_conj((lay_ref[k, 0], lay_ref[k, 1]), back)

    def behind(slots):
        illum = (probe_ref[0], probe_ref[1])
        for k, back in zip(slots, apply(SPREAD_ADJ, [(lay_ref[k, 0], lay_ref[k, 1]) for k in slots])):
            put(k, product_conj(illum, back))

    def gather(s):
        def step(block, carry):
            at = block * 8
            sums = [jnp.zeros((8, N), F32)] * (2 * LANES)
            for k in range(SLOTS):
                from_row = jnp.clip(at - lax.rem(pos_ref[0, k], T) + 8, 0, GROWS - 8)
                sums = [
                    total + grad_ref[k, i // LANES, i % LANES, pl.ds(from_row, 8), :]
                    for i, total in enumerate(sums)
                ]
            for i, total in enumerate(sums):
                acc[s][i // LANES, i % LANES, pl.ds(pl.multiple_of(at, 8), 8), :] = total
            return carry

        lax.fori_loop(0, E // 8, step, 0)

    def mid_start(s):
        rows = [
            copy(acc[s].at[:, :, 0:N, :], down_ref.at[s], up),
            copy(acc[s].at[:, :, T:E, :], up_ref.at[s], down),
        ]
        cols = [
            copy(acc[s].at[:, 0, N:T, :], right_ref.at[s, :, N:T, :], left),
            copy(acc[s].at[:, 2, N:T, :], left_ref.at[s, :, N:T, :], right),
        ]
        return rows, cols

    def mid_next(s, copies):
        rows, cols = copies
        wait(rows)
        acc[s][:, :, 0:N, :] = acc[s][:, :, 0:N, :] + jnp.where(has_up, up_ref[s], 0.0)
        acc[s][:, :, T:E, :] = acc[s][:, :, T:E, :] + jnp.where(has_down, down_ref[s], 0.0)
        for part in (slice(0, N), slice(T, E)):
            cols = cols + [
                copy(acc[s].at[:, 0, part, :], right_ref.at[s, :, part, :], left),
                copy(acc[s].at[:, 2, part, :], left_ref.at[s, :, part, :], right),
            ]
        return cols

    def mid_end(s, cols):
        wait(cols)
        inside = ((low == False) | has_left, (low == low), low | has_right)
        for c in range(2):
            for t in range(LANES):
                for b in range(LANES):
                    part = slice(b * N, b * N + N)
                    value = ext[s][c, t, part, :] - acc[s][c, t, part, :]
                    if t == 0:
                        value = value - jnp.where(has_left, left_ref[s, c, part, :], 0.0)
                    if t == 2:
                        value = value - jnp.where(has_right, right_ref[s, c, part, :], 0.0)
                    if t != 1:
                        value = jnp.where(inside[t], value, 0.0)
                    if b != 1:
                        line = lax.broadcasted_iota(jnp.int32, (N, N), 0)
                        keep = ((line >= HALF) | has_up) if b == 0 else ((line < HALF) | has_down)
                        value = jnp.where(keep, value, 0.0)
                    ext[s][c, t, part, :] = value

    def fin_start(s):
        return [
            copy(acc[s].at[:, :, 0:HALF, :], fin_down.at[s], up),
            copy(acc[s].at[:, :, E - HALF : E, :], fin_up.at[s], down),
        ]

    def fin_next(s, rows):
        wait(rows)
        head, tail = slice(HALF, N), slice(T, T + HALF)
        acc[s][:, :, head, :] = acc[s][:, :, head, :] + jnp.where(has_up, fin_up[s], 0.0)
        acc[s][:, :, tail, :] = acc[s][:, :, tail, :] + jnp.where(has_down, fin_down[s], 0.0)
        own = slice(HALF, HALF + T)
        fin_src[s, 0] = jnp.where(low_t, acc[s][0, 0, own, :], swap(acc[s][1, 0, own, :]))
        fin_src[s, 1] = jnp.where(low_t, swap(acc[s][1, 2, own, :]), acc[s][0, 2, own, :])
        return [copy(fin_src.at[s, 0], fin_dst.at[s, 1], left), copy(fin_src.at[s, 1], fin_dst.at[s, 0], right)]

    def fin_end(s, cols):
        wait(cols)
        own = slice(HALF, HALF + T)
        from_left = jnp.where(has_left, fin_dst[s, 0], 0.0)
        from_right = jnp.where(has_right, fin_dst[s, 1], 0.0)
        for c in range(2):
            mine = [ext[s][c, t, own, :] - acc[s][c, t, own, :] for t in range(LANES)]
            begin = swap(mine[0] - (from_left if c == 0 else swap(from_left)))
            middle = swap(mine[1])
            end = swap(mine[2] - (from_right if c == 0 else swap(from_right)))
            out_ref[s, c, :, 0:N] = jnp.where(low_t, begin, middle)
            out_ref[s, c, :, N : 2 * N] = jnp.where(low_t, middle, end)

    border(0)
    loop(ahead, 0, SLOTS)
    border(1)
    loop(detect, 0, SLOTS)
    gather(1)
    one = mid_start(1)
    loop(behind, 0, SLOTS // 2)
    one = mid_next(1, one)
    loop(behind, SLOTS // 2, SLOTS)
    gather(0)
    mid_end(0, mid_next(0, mid_start(0)))

    loop(ahead, 0, SLOTS)
    mid_end(1, one)
    loop(detect, 0, SLOTS)
    gather(1)
    one = fin_start(1)
    loop(behind, 0, SLOTS // 2)
    one = fin_next(1, one)
    loop(behind, SLOTS // 2, SLOTS)
    gather(0)
    zero = fin_next(0, fin_start(0))
    fin_end(1, one)
    fin_end(0, zero)


COPIES = 32


def solution(mesh):
    rows_n, cols_n = mesh.shape["row"], mesh.shape["col"]
    vmem = pl.BlockSpec(memory_space=pltpu.VMEM)
    smem = pl.BlockSpec(memory_space=pltpu.SMEM)

    def body(object_slices, probe, amplitudes, scan_pos, scan_count):
        tab = jnp.asarray(tables())
        call = pl.pallas_call(
            functools.partial(kernel, rows_n, cols_n),
            out_shape=jax.ShapeDtypeStruct(object_slices.shape, F32),
            in_specs=[smem, smem, vmem, vmem, vmem, vmem],
            out_specs=vmem,
            scratch_shapes=[
                pltpu.VMEM((2, LANES, E, N), F32),
                pltpu.VMEM((2, LANES, E, N), F32),
                pltpu.VMEM((2, LANES, E, N), F32),
                pltpu.VMEM((2, LANES, E, N), F32),
                pltpu.VMEM((SLOTS, 2, N, N), F32),
                pltpu.VMEM((SLOTS, 2, N, N), F32),
                pltpu.VMEM((SLOTS, 2, LANES, GROWS, N), F32),
                pltpu.VMEM((2, 2, T, N), F32),
                pltpu.VMEM((2, 2, T, N), F32),
                pltpu.VMEM((2, 2, LANES, N, N), F32),
                pltpu.VMEM((2, 2, LANES, N, N), F32),
                pltpu.VMEM((2, 2, E, N), F32),
                pltpu.VMEM((2, 2, E, N), F32),
                pltpu.VMEM((2, 2, LANES, HALF, N), F32),
                pltpu.VMEM((2, 2, LANES, HALF, N), F32),
                pltpu.VMEM((2, 2, T, N), F32),
                pltpu.VMEM((2, 2, T, N), F32),
                pltpu.SemaphoreType.DMA((COPIES,)),
                pltpu.SemaphoreType.DMA((COPIES,)),
            ],
            compiler_params=pltpu.CompilerParams(
                collective_id=0, has_side_effects=True, vmem_limit_bytes=56 * 2**20
            ),
        )
        return call(
            scan_pos.reshape(2, SLOTS), scan_count, object_slices, probe,
            amplitudes.reshape(SLOTS, N, N), tab,
        )

    in_specs = (
        P(None, None, "row", "col"),
        P(),
        P("row", "col", None, None, None),
        P(None, "row", "col", None),
        P("row", "col"),
    )
    out_specs = P(None, None, "row", "col")
    return jax.shard_map(body, mesh=mesh, in_specs=in_specs, out_specs=out_specs, check_vma=False)
```

```python
import functools
import math

import jax
import jax.numpy as jnp
import numpy as np
from jax import lax
from jax.experimental import pallas as pl
from jax.experimental.pallas import tpu as pltpu
from jax.sharding import PartitionSpec as P

ITERS = 2
MESH = pl.DeviceIdType.MESH
F32 = jnp.float32
BF16 = jnp.bfloat16

modulus_offset = 0.5
fresnel_scale = 0.9

N = 128
T = 256
E = T + N
HALF = N // 2
LANES = E // N
SLOTS = 16
GROUP = 8
STRIP = 32
GROWS = N + 2 * STRIP


def tables():
    positions = np.arange(N)
    frequency = np.where(positions < N // 2, positions, positions - N).astype(np.float64)
    angle = -2.0 * math.pi / N * (np.outer(positions, positions) % N)
    dft = (np.cos(angle) + 1j * np.sin(angle)) / math.sqrt(N)
    phase = math.pi * fresnel_scale * frequency**2 / N
    spread = np.conj(dft) @ (np.exp(1j * phase)[:, None] * dft)
    spread = 0.5 * (spread + spread.T)
    made = []
    for matrix in (spread, dft):
        left = np.block([[matrix.real, -matrix.imag], [matrix.imag, matrix.real]])
        for form in (left, left.T):
            high = form.astype(np.float32).astype(BF16)
            low = (form - high.astype(np.float64)).astype(np.float32).astype(BF16)
            made += [high, low]
    return np.stack(made)


def split(value):
    high = value.astype(BF16)
    return high, (value - high.astype(F32)).astype(BF16)


def dot(a, b):
    return jnp.dot(a, b, preferred_element_type=F32)


def kernel(
    rows_n, cols_n,
    pos_ref, count_ref, obj_ref, probe_ref, amps_ref, tab_ref,
    out_ref,
    ext0, ext1, acc0, acc1, inc_ref, lay_ref, grad_ref, mask_ref,
    halo_src, halo_dst, up_ref, down_ref, left_ref, right_ref,
    fin_up, fin_down, fin_src, fin_dst,
    send_sem, recv_sem,
):
    row, col = lax.axis_index("row"), lax.axis_index("col")
    up = (lax.rem(row + rows_n - 1, rows_n), col)
    down = (lax.rem(row + 1, rows_n), col)
    left = (row, lax.rem(col + cols_n - 1, cols_n))
    right = (row, lax.rem(col + 1, cols_n))
    has_up, has_down = row > 0, row < rows_n - 1
    has_left, has_right = col > 0, col < cols_n - 1
    ext, acc = (ext0, ext1), (acc0, acc1)
    used = [0]

    barrier = pltpu.get_barrier_semaphore()
    for device in (up, down, left, right):
        pl.semaphore_signal(barrier, inc=1, device_id=device, device_id_type=MESH)

    def copy(source, target, device):
        index = used[0]
        used[0] += 1
        made = pltpu.make_async_remote_copy(
            src_ref=source, dst_ref=target, send_sem=send_sem.at[index],
            recv_sem=recv_sem.at[index], device_id=device, device_id_type=MESH,
        )
        made.start()
        return made

    def wait(copies):
        for made in copies:
            made.wait()

    lane = lax.broadcasted_iota(jnp.int32, (N, N), 1)
    low = lane < HALF

    def swap(value):
        return pltpu.roll(value, HALF, 1)

    low_t = lax.broadcasted_iota(jnp.int32, (T, N), 1) < HALF
    for s in range(2):
        first = [obj_ref[s, c, :, 0:N] for c in range(2)]
        last = [obj_ref[s, c, :, N : 2 * N] for c in range(2)]
        halo_src[s, 0] = jnp.where(low_t, first[1], swap(first[0]))
        halo_src[s, 1] = jnp.where(low_t, swap(last[0]), last[1])

    pl.semaphore_wait(barrier, 4)
    side = [
        [copy(halo_src.at[s, 0], halo_dst.at[s, 1], left), copy(halo_src.at[s, 1], halo_dst.at[s, 0], right)]
        for s in range(2)
    ]

    for s in range(2):
        for c in range(2):
            first, last = swap(obj_ref[s, c, :, 0:N]), swap(obj_ref[s, c, :, N : 2 * N])
            ext[s][c, 1, HALF : HALF + T, :] = jnp.where(low_t, first, last)

    def place(k):
        at_row, at_col = lax.rem(pos_ref[0, k], T), lax.rem(pos_ref[1, k], T)
        return at_row, at_col // N, at_col % N

    def prepare(k, carry):
        _, at_lane, shift = place(k)
        live = (k < count_ref[0, 0]).astype(F32)
        second = live * at_lane.astype(F32)
        first = live - second
        upper = (lax.broadcasted_iota(jnp.int32, (8, N), 1) >= shift).astype(F32)
        mask_ref[k, 0] = upper * first
        mask_ref[k, 1] = upper * second + (1.0 - upper) * first
        mask_ref[k, 2] = (1.0 - upper) * second
        for c in range(2):
            grad_ref[k, c, 0:STRIP, :] = jnp.zeros((STRIP, N), F32)
            grad_ref[k, c, GROWS - STRIP : GROWS, :] = jnp.zeros((STRIP, N), F32)
        return carry

    lax.fori_loop(0, SLOTS, prepare, 0)

    edge = []
    for s in range(2):
        wait(side[s])
        from_left = jnp.where(has_left, halo_dst[s, 0], 0.0)
        from_right = jnp.where(has_right, halo_dst[s, 1], 0.0)
        for c in range(2):
            first, last = swap(obj_ref[s, c, :, 0:N]), swap(obj_ref[s, c, :, N : 2 * N])
            ext[s][c, 0, HALF : HALF + T, :] = jnp.where(low_t, from_left if c == 0 else swap(from_left), first)
            ext[s][c, 2, HALF : HALF + T, :] = jnp.where(low_t, last, from_right if c == 0 else swap(from_right))
        edge.append([
            copy(ext[s].at[:, :, HALF : 2 * HALF, :], ext[s].at[:, :, E - HALF : E, :], up),
            copy(ext[s].at[:, :, T : T + HALF, :], ext[s].at[:, :, 0:HALF, :], down),
        ])

    def border(s):
        wait(edge[s])
        ext[s][:, :, 0:HALF, :] = jnp.where(has_up, ext[s][:, :, 0:HALF, :], 0.0)
        ext[s][:, :, E - HALF : E, :] = jnp.where(has_down, ext[s][:, :, E - HALF : E, :], 0.0)

    def patch(s, k):
        at_row, at_lane, shift = place(k)
        back = (N - shift) % N
        parts = []
        for c in range(2):
            here = ext[s][c, at_lane, pl.ds(at_row, N), :]
            after = ext[s][c, at_lane + 1, pl.ds(at_row, N), :]
            parts.append(pltpu.roll(jnp.where(lane >= shift, here, after), back, 1))
        return parts

    def put(k, parts):
        _, _, shift = place(k)
        for c in range(2):
            grad_ref[k, c, STRIP : STRIP + N, :] = pltpu.roll(parts[c], shift, 1)

    def tall(parts):
        return jnp.concatenate(parts, axis=0)

    def wide(parts):
        return jnp.concatenate(parts, axis=1)

    def apply(which, waves):
        high_l, low_l = tab_ref[2 * which], tab_ref[2 * which + 1]
        other = which ^ 1
        high_r, low_r = tab_ref[2 * other], tab_ref[2 * other + 1]
        high, low_part = split(tall([wide([wave[c] for wave in waves]) for c in range(2)]))
        mid = dot(wide([high_l, high_l, low_l]), tall([high, low_part, high]))
        high, low_part = split(
            tall([wide([mid[:N, i * N : i * N + N], mid[N:, i * N : i * N + N]]) for i in range(len(waves))])
        )
        done = dot(wide([high, low_part, high]), tall([high_r, high_r, low_r]))
        return [(done[i * N : i * N + N, :N], done[i * N : i * N + N, N:]) for i in range(len(waves))]

    def product(a, b):
        return a[0] * b[0] - a[1] * b[1], a[0] * b[1] + a[1] * b[0]

    def product_conj(a, b):
        return a[0] * b[0] + a[1] * b[1], a[0] * b[1] - a[1] * b[0]

    SPREAD, SPREAD_ADJ, DFT, DFT_INV = 0, 1, 2, 3

    def loop(stage):
        for start in range(0, SLOTS, GROUP):
            stage(range(start, start + GROUP))

    def ahead(slots):
        illum = (probe_ref[0], probe_ref[1])
        waves = apply(SPREAD, [product(illum, patch(0, k)) for k in slots])
        for k, wave in zip(slots, waves):
            inc_ref[k, 0], inc_ref[k, 1] = wave

    def detect(slots):
        exits = []
        for k in slots:
            layer = patch(1, k)
            lay_ref[k, 0], lay_ref[k, 1] = layer
            exits.append(product((inc_ref[k, 0], inc_ref[k, 1]), layer))
        residuals = []
        for k, (re, im) in zip(slots, apply(DFT, exits)):
            factor = 1.0 - amps_ref[k] / jnp.sqrt(re * re + im * im + modulus_offset)
            residuals.append((re * factor, im * factor))
        for k, back in zip(slots, apply(DFT_INV, residuals)):
            put(k, product_conj((inc_ref[k, 0], inc_ref[k, 1]), back))
            lay_ref[k, 0], lay_ref[k, 1] = product_conj((lay_ref[k, 0], lay_ref[k, 1]), back)

    def behind(slots):
        illum = (probe_ref[0], probe_ref[1])
        for k, back in zip(slots, apply(SPREAD_ADJ, [(lay_ref[k, 0], lay_ref[k, 1]) for k in slots])):
            put(k, product_conj(illum, back))

    def gather(s):
        def step(block, carry):
            at = block * STRIP
            sums = [jnp.zeros((STRIP, N), F32)] * (2 * LANES)
            for k in range(SLOTS):
                from_row = jnp.clip(at - lax.rem(pos_ref[0, k], T) + STRIP, 0, GROWS - STRIP)
                keep = [tall([mask_ref[k, t]] * (STRIP // 8)) for t in range(LANES)]
                for c in range(2):
                    part = grad_ref[k, c, pl.ds(from_row, STRIP), :]
                    for t in range(LANES):
                        sums[c * LANES + t] = sums[c * LANES + t] + part * keep[t]
            for i, total in enumerate(sums):
                acc[s][i // LANES, i % LANES, pl.ds(pl.multiple_of(at, STRIP), STRIP), :] = total
            return carry

        lax.fori_loop(0, E // STRIP, step, 0)

    def mid_start(s):
        rows = [
            copy(acc[s].at[:, :, 0:N, :], down_ref.at[s], up),
            copy(acc[s].at[:, :, T:E, :], up_ref.at[s], down),
        ]
        cols = [
            copy(acc[s].at[:, 0, N:T, :], right_ref.at[s, :, N:T, :], left),
            copy(acc[s].at[:, 2, N:T, :], left_ref.at[s, :, N:T, :], right),
        ]
        return rows, cols

    def mid_next(s, copies):
        rows, cols = copies
        wait(rows)
        acc[s][:, :, 0:N, :] = acc[s][:, :, 0:N, :] + jnp.where(has_up, up_ref[s], 0.0)
        acc[s][:, :, T:E, :] = acc[s][:, :, T:E, :] + jnp.where(has_down, down_ref[s], 0.0)
        for part in (slice(0, N), slice(T, E)):
            cols = cols + [
                copy(acc[s].at[:, 0, part, :], right_ref.at[s, :, part, :], left),
                copy(acc[s].at[:, 2, part, :], left_ref.at[s, :, part, :], right),
            ]
        return cols

    def mid_end(s, cols):
        wait(cols)
        inside = ((low == False) | has_left, (low == low), low | has_right)
        for c in range(2):
            for t in range(LANES):
                for b in range(LANES):
                    part = slice(b * N, b * N + N)
                    value = ext[s][c, t, part, :] - acc[s][c, t, part, :]
                    if t == 0:
                        value = value - jnp.where(has_left, left_ref[s, c, part, :], 0.0)
                    if t == 2:
                        value = value - jnp.where(has_right, right_ref[s, c, part, :], 0.0)
                    if t != 1:
                        value = jnp.where(inside[t], value, 0.0)
                    if b != 1:
                        line = lax.broadcasted_iota(jnp.int32, (N, N), 0)
                        keep = ((line >= HALF) | has_up) if b == 0 else ((line < HALF) | has_down)
                        value = jnp.where(keep, value, 0.0)
                    ext[s][c, t, part, :] = value

    def fin_start(s):
        return [
            copy(acc[s].at[:, :, 0:HALF, :], fin_down.at[s], up),
            copy(acc[s].at[:, :, E - HALF : E, :], fin_up.at[s], down),
        ]

    def fin_next(s, rows):
        wait(rows)
        head, tail = slice(HALF, N), slice(T, T + HALF)
        acc[s][:, :, head, :] = acc[s][:, :, head, :] + jnp.where(has_up, fin_up[s], 0.0)
        acc[s][:, :, tail, :] = acc[s][:, :, tail, :] + jnp.where(has_down, fin_down[s], 0.0)
        own = slice(HALF, HALF + T)
        fin_src[s, 0] = jnp.where(low_t, acc[s][0, 0, own, :], swap(acc[s][1, 0, own, :]))
        fin_src[s, 1] = jnp.where(low_t, swap(acc[s][1, 2, own, :]), acc[s][0, 2, own, :])
        return [copy(fin_src.at[s, 0], fin_dst.at[s, 1], left), copy(fin_src.at[s, 1], fin_dst.at[s, 0], right)]

    def fin_end(s, cols):
        wait(cols)
        own = slice(HALF, HALF + T)
        from_left = jnp.where(has_left, fin_dst[s, 0], 0.0)
        from_right = jnp.where(has_right, fin_dst[s, 1], 0.0)
        for c in range(2):
            mine = [ext[s][c, t, own, :] - acc[s][c, t, own, :] for t in range(LANES)]
            begin = swap(mine[0] - (from_left if c == 0 else swap(from_left)))
            middle = swap(mine[1])
            end = swap(mine[2] - (from_right if c == 0 else swap(from_right)))
            out_ref[s, c, :, 0:N] = jnp.where(low_t, begin, middle)
            out_ref[s, c, :, N : 2 * N] = jnp.where(low_t, middle, end)

    border(0)
    loop(ahead)
    border(1)
    loop(detect)
    gather(1)
    one = mid_start(1)
    loop(behind)
    gather(0)
    zero = mid_start(0)
    one = mid_next(1, one)
    mid_end(0, mid_next(0, zero))

    loop(ahead)
    mid_end(1, one)
    loop(detect)
    gather(1)
    one = fin_start(1)
    loop(behind)
    gather(0)
    zero = fin_start(0)
    one = fin_next(1, one)
    zero = fin_next(0, zero)
    fin_end(1, one)
    fin_end(0, zero)


COPIES = 32


def solution(mesh):
    rows_n, cols_n = mesh.shape["row"], mesh.shape["col"]
    vmem = pl.BlockSpec(memory_space=pltpu.VMEM)
    smem = pl.BlockSpec(memory_space=pltpu.SMEM)

    def body(object_slices, probe, amplitudes, scan_pos, scan_count):
        tab = jnp.asarray(tables())
        call = pl.pallas_call(
            functools.partial(kernel, rows_n, cols_n),
            out_shape=jax.ShapeDtypeStruct(object_slices.shape, F32),
            in_specs=[smem, smem, vmem, vmem, vmem, vmem],
            out_specs=vmem,
            scratch_shapes=[
                pltpu.VMEM((2, LANES, E, N), F32),
                pltpu.VMEM((2, LANES, E, N), F32),
                pltpu.VMEM((2, LANES, E, N), F32),
                pltpu.VMEM((2, LANES, E, N), F32),
                pltpu.VMEM((SLOTS, 2, N, N), F32),
                pltpu.VMEM((SLOTS, 2, N, N), F32),
                pltpu.VMEM((SLOTS, 2, GROWS, N), F32),
                pltpu.VMEM((SLOTS, LANES, 8, N), F32),
                pltpu.VMEM((2, 2, T, N), F32),
                pltpu.VMEM((2, 2, T, N), F32),
                pltpu.VMEM((2, 2, LANES, N, N), F32),
                pltpu.VMEM((2, 2, LANES, N, N), F32),
                pltpu.VMEM((2, 2, E, N), F32),
                pltpu.VMEM((2, 2, E, N), F32),
                pltpu.VMEM((2, 2, LANES, HALF, N), F32),
                pltpu.VMEM((2, 2, LANES, HALF, N), F32),
                pltpu.VMEM((2, 2, T, N), F32),
                pltpu.VMEM((2, 2, T, N), F32),
                pltpu.SemaphoreType.DMA((COPIES,)),
                pltpu.SemaphoreType.DMA((COPIES,)),
            ],
            compiler_params=pltpu.CompilerParams(
                collective_id=0, has_side_effects=True, vmem_limit_bytes=56 * 2**20
            ),
        )
        return call(
            scan_pos.reshape(2, SLOTS), scan_count, object_slices, probe,
            amplitudes.reshape(SLOTS, N, N), tab,
        )

    in_specs = (
        P(None, None, "row", "col"),
        P(),
        P("row", "col", None, None, None),
        P(None, "row", "col", None),
        P("row", "col"),
    )
    out_specs = P(None, None, "row", "col")
    return jax.shard_map(body, mesh=mesh, in_specs=in_specs, out_specs=out_specs, check_vma=False)
```

```python
import functools
import math

import jax
import jax.numpy as jnp
import numpy as np
from jax import lax
from jax.experimental import pallas as pl
from jax.experimental.pallas import tpu as pltpu
from jax.sharding import PartitionSpec as P

ITERS = 2
MESH = pl.DeviceIdType.MESH
F32 = jnp.float32
BF16 = jnp.bfloat16

modulus_offset = 0.5
fresnel_scale = 0.9

N = 128
T = 256
E = T + N
HALF = N // 2
LANES = E // N
SLOTS = 16
GROUP = 8
STRIP = 64
SHIFTED = N + 8
GROWS = SHIFTED + 2 * STRIP


def tables():
    positions = np.arange(N)
    frequency = np.where(positions < N // 2, positions, positions - N).astype(np.float64)
    angle = -2.0 * math.pi / N * (np.outer(positions, positions) % N)
    dft = (np.cos(angle) + 1j * np.sin(angle)) / math.sqrt(N)
    phase = math.pi * fresnel_scale * frequency**2 / N
    spread = np.conj(dft) @ (np.exp(1j * phase)[:, None] * dft)
    spread = 0.5 * (spread + spread.T)
    made = []
    for matrix in (spread, dft):
        left = np.block([[matrix.real, -matrix.imag], [matrix.imag, matrix.real]])
        for form in (left, left.T):
            high = form.astype(np.float32).astype(BF16)
            low = (form - high.astype(np.float64)).astype(np.float32).astype(BF16)
            made += [high, low]
    return np.stack(made)


def split(value):
    high = value.astype(BF16)
    return high, (value - high.astype(F32)).astype(BF16)


def dot(a, b):
    return jnp.dot(a, b, preferred_element_type=F32)


def kernel(
    rows_n, cols_n,
    pos_ref, count_ref, obj_hbm, probe_hbm, amps_hbm, tab_hbm,
    out_hbm,
    obj_ref, probe_ref, amps_ref, tab_ref, out_ref,
    ext0, ext1, acc0, acc1, inc_ref, lay_ref, grad0, grad1, mask_ref,
    halo_src, halo_dst, fin_src, fin_dst, up_ref, down_ref,
    send_sem, recv_sem, local_sem,
):
    row, col = lax.axis_index("row"), lax.axis_index("col")
    above, below = lax.rem(row + rows_n - 1, rows_n), lax.rem(row + 1, rows_n)
    before, behind_col = lax.rem(col + cols_n - 1, cols_n), lax.rem(col + 1, cols_n)
    up, down, left, right = (above, col), (below, col), (row, before), (row, behind_col)
    corners = (((above, before), (below, before)), ((above, behind_col), (below, behind_col)))
    has_up, has_down = row > 0, row < rows_n - 1
    has_left, has_right = col > 0, col < cols_n - 1
    ext, acc, grads = (ext0, ext1), (acc0, acc1), (grad0, grad1)
    used = [0]

    barrier = pltpu.get_barrier_semaphore()
    for device in (*corners[0], *corners[1], left, right, up, down):
        pl.semaphore_signal(barrier, inc=1, device_id=device, device_id_type=MESH)

    def load(source, target, index):
        made = pltpu.make_async_copy(source, target, local_sem.at[index])
        made.start()
        return made

    object_in = [load(obj_hbm.at[s], obj_ref.at[s], s) for s in range(2)]
    probe_in = load(probe_hbm, probe_ref, 2)
    tab_in = load(tab_hbm, tab_ref, 3)
    amps_in = load(amps_hbm, amps_ref, 4)

    def copy(source, target, device):
        index = used[0]
        used[0] += 1
        made = pltpu.make_async_remote_copy(
            src_ref=source, dst_ref=target, send_sem=send_sem.at[index],
            recv_sem=recv_sem.at[index], device_id=device, device_id_type=MESH,
        )
        made.start()
        return made

    def wait(copies):
        for made in copies:
            made.wait()

    lane = lax.broadcasted_iota(jnp.int32, (N, N), 1)

    def swap(value):
        return pltpu.roll(value, HALF, 1)

    def lows(value):
        return lax.broadcasted_iota(jnp.int32, value.shape, 1) < HALF

    def pick(in_low, in_high):
        return jnp.where(lows(in_low), in_low, in_high)

    def place(k):
        at_row, at_col = pos_ref[0, k], pos_ref[1, k]
        return (at_row >> 3) & (T // 8 - 1), at_row & 7, (at_col >> 7) & 1, at_col & (N - 1)

    def prepare(k, carry):
        _, _, at_lane, shift = place(k)
        live = (k < count_ref[0, 0]).astype(F32)
        upper = (lax.broadcasted_iota(jnp.int32, (8, N), 1) >= shift).astype(F32)
        mask_ref[k, 0] = upper * live
        mask_ref[k, 1] = (1.0 - upper) * live
        mask_ref[k, 2] = jnp.zeros((8, N), F32) + (1 - at_lane).astype(F32)
        for c in range(2):
            for half in range(2):
                for grad in grads:
                    grad[k, c, half, 0:STRIP, :] = jnp.zeros((STRIP, N), F32)
                    grad[k, c, half, GROWS - STRIP : GROWS, :] = jnp.zeros((STRIP, N), F32)
        return carry

    own, head, tail = slice(HALF, HALF + T), slice(0, HALF), slice(HALF + T, E)

    def edges(source, target, s):
        made = []
        begin = source.shape[2] - T
        first, last, whole = slice(0, HALF), slice(source.shape[2] - HALF, source.shape[2]), slice(begin // 2, begin // 2 + T)
        for side in range(2):
            made.append(copy(source.at[s, side, first], target.at[s, 1 - side, tail], corners[side][0]))
            made.append(copy(source.at[s, side, last], target.at[s, 1 - side, head], corners[side][1]))
        for side, device in enumerate((left, right)):
            made.append(copy(source.at[s, side, whole], target.at[s, 1 - side, own], device))
        return made

    def halo_pack(s):
        halo_src[s, 0] = pick(swap(ext[s][1, 0, own, :]), ext[s][0, 0, own, :])
        halo_src[s, 1] = pick(ext[s][0, 2, own, :], swap(ext[s][1, 2, own, :]))

    def halo_start(s):
        return edges(halo_src, halo_dst, s) + [
            copy(ext[s].at[:, :, HALF : 2 * HALF, :], ext[s].at[:, :, tail, :], up),
            copy(ext[s].at[:, :, T : T + HALF, :], ext[s].at[:, :, head, :], down),
        ]

    def halo_end(s, copies):
        wait(copies)
        for part, inside in ((head, has_up), (own, None), (tail, has_down)):
            for t in range(LANES):
                if t == 1 and inside is None:
                    continue
                for c in range(2):
                    value = ext[s][c, t, part, :]
                    if t != 1:
                        strip = jnp.where((has_left, None, has_right)[t], halo_dst[s, t // 2, part, :], 0.0)
                        strip = strip if c == 0 else swap(strip)
                        value = pick(strip, value) if t == 0 else pick(value, strip)
                    ext[s][c, t, part, :] = value if inside is None else jnp.where(inside, value, 0.0)

    def grad_start(s):
        fin_src[s, 0] = pick(acc[s][0, 0], swap(acc[s][1, 0]))
        fin_src[s, 1] = pick(swap(acc[s][1, 2]), acc[s][0, 2])
        return edges(fin_src, fin_dst, s) + [
            copy(acc[s].at[:, :, head, :], down_ref.at[s], up),
            copy(acc[s].at[:, :, tail, :], up_ref.at[s], down),
        ]

    def grad_end(s, copies, last):
        wait(copies)
        for p in range(T // HALF):
            part = slice(HALF * (p + 1), HALF * (p + 2))
            strips = []
            for side, there in enumerate((has_left, has_right)):
                strip = fin_dst[s, side, part, :]
                if p == 0:
                    strip = strip + jnp.where(has_up, fin_dst[s, side, head, :], 0.0)
                if p == T // HALF - 1:
                    strip = strip + jnp.where(has_down, fin_dst[s, side, tail, :], 0.0)
                strips.append(jnp.where(there, strip, 0.0))
            for c in range(2):
                made = []
                for t in range(LANES):
                    value = ext[s][c, t, part, :] - acc[s][c, t, part, :]
                    if t != 1:
                        value = value - (strips[t // 2] if c == 0 else swap(strips[t // 2]))
                    if p == 0:
                        value = value - jnp.where(has_up, up_ref[s, c, t], 0.0)
                    if p == T // HALF - 1:
                        value = value - jnp.where(has_down, down_ref[s, c, t], 0.0)
                    made.append(value)
                if last:
                    made = [swap(value) for value in made]
                    out_ref[s, c, HALF * p : HALF * (p + 1), 0:N] = pick(made[0], made[1])
                    out_ref[s, c, HALF * p : HALF * (p + 1), N : 2 * N] = pick(made[1], made[2])
                else:
                    for t in range(LANES):
                        ext[s][c, t, part, :] = made[t]

    def patch(s, k):
        eighth, over, at_lane, shift = place(k)
        rows = pl.ds(eighth * 8, SHIFTED)
        parts = []
        for c in range(2):
            here, after = ext[s][c, at_lane, rows, :], ext[s][c, at_lane + 1, rows, :]
            both = jnp.where(lax.broadcasted_iota(jnp.int32, (SHIFTED, N), 1) >= shift, here, after)
            both = pltpu.roll(both, 8 - over, 0)[SHIFTED - N :]
            parts.append(pltpu.roll(both, (N - shift) & (N - 1), 1))
        return parts

    def put(s, k, parts):
        _, over, _, shift = place(k)
        for c in range(2):
            moved = tall([pltpu.roll(parts[c], shift, 1), jnp.zeros((SHIFTED - N, N), F32)])
            moved = pltpu.roll(moved, over, 0)
            for half in range(2):
                grads[s][k, c, half, STRIP : STRIP + SHIFTED, :] = moved * tall([mask_ref[k, half]] * (SHIFTED // 8))

    def tall(parts):
        return jnp.concatenate(parts, axis=0)

    def wide(parts):
        return jnp.concatenate(parts, axis=1)

    def apply(which, waves):
        high_l, low_l = tab_ref[2 * which], tab_ref[2 * which + 1]
        other = which ^ 1
        high_r, low_r = tab_ref[2 * other], tab_ref[2 * other + 1]
        high, low_part = split(tall([wide([wave[c] for wave in waves]) for c in range(2)]))
        mid = dot(wide([high_l, high_l, low_l]), tall([high, low_part, high]))
        high, low_part = split(
            tall([wide([mid[:N, i * N : i * N + N], mid[N:, i * N : i * N + N]]) for i in range(len(waves))])
        )
        done = dot(wide([high, low_part, high]), tall([high_r, high_r, low_r]))
        return [(done[i * N : i * N + N, :N], done[i * N : i * N + N, N:]) for i in range(len(waves))]

    def product(a, b):
        return a[0] * b[0] - a[1] * b[1], a[0] * b[1] + a[1] * b[0]

    def product_conj(a, b):
        return a[0] * b[0] + a[1] * b[1], a[0] * b[1] - a[1] * b[0]

    SPREAD, SPREAD_ADJ, DFT, DFT_INV = 0, 1, 2, 3

    def loop(stage):
        for start in range(0, SLOTS, GROUP):
            stage(range(start, start + GROUP))

    def ahead(slots):
        illum = (probe_ref[0], probe_ref[1])
        waves = apply(SPREAD, [product(illum, patch(0, k)) for k in slots])
        for k, wave in zip(slots, waves):
            inc_ref[k, 0], inc_ref[k, 1] = wave

    def detect(slots):
        exits = []
        for k in slots:
            layer = patch(1, k)
            lay_ref[k, 0], lay_ref[k, 1] = layer
            exits.append(product((inc_ref[k, 0], inc_ref[k, 1]), layer))
        residuals = []
        for k, (re, im) in zip(slots, apply(DFT, exits)):
            factor = 1.0 - amps_ref[k] / jnp.sqrt(re * re + im * im + modulus_offset)
            residuals.append((re * factor, im * factor))
        for k, back in zip(slots, apply(DFT_INV, residuals)):
            put(1, k, product_conj((inc_ref[k, 0], inc_ref[k, 1]), back))
            lay_ref[k, 0], lay_ref[k, 1] = product_conj((lay_ref[k, 0], lay_ref[k, 1]), back)

    def behind(slots):
        illum = (probe_ref[0], probe_ref[1])
        for k, back in zip(slots, apply(SPREAD_ADJ, [(lay_ref[k, 0], lay_ref[k, 1]) for k in slots])):
            put(0, k, product_conj(illum, back))

    def strips_of(s, k, half, at):
        from_row = jnp.clip(at - place(k)[0] + STRIP // 8, 0, (GROWS - STRIP) // 8) * 8
        return [grads[s][k, c, half, pl.ds(from_row, STRIP), :] for c in range(2)]

    def gather_sides(s):
        def step(block, carry):
            at = block * STRIP
            both = [jnp.zeros((STRIP, N), F32)] * 2
            first = [jnp.zeros((STRIP, N), F32)] * 2
            for k in range(SLOTS):
                keep = tall([mask_ref[k, 2]] * (STRIP // 8))
                for c, part in enumerate(strips_of(s, k, place(k)[2], block * (STRIP // 8))):
                    both[c] = both[c] + part
                    first[c] = first[c] + part * keep
            for c in range(2):
                acc[s][c, 0, pl.ds(pl.multiple_of(at, STRIP), STRIP), :] = first[c]
                acc[s][c, 2, pl.ds(pl.multiple_of(at, STRIP), STRIP), :] = both[c] - first[c]
            return carry

        lax.fori_loop(0, E // STRIP, step, 0)

    def gather_middle(s, number, strip_at):
        def step(block, carry):
            at = strip_at(block) * STRIP
            total = [jnp.zeros((STRIP, N), F32)] * 2
            for k in range(SLOTS):
                for c, part in enumerate(strips_of(s, k, 1 - place(k)[2], strip_at(block) * (STRIP // 8))):
                    total[c] = total[c] + part
            for c in range(2):
                acc[s][c, 1, pl.ds(pl.multiple_of(at, STRIP), STRIP), :] = total[c]
            return carry

        lax.fori_loop(0, number, step, 0)

    def exchange(s):
        rim = HALF // STRIP
        gather_middle(s, 2 * rim, lambda i: i + (i // rim) * (T // STRIP))
        gather_sides(s)
        made = grad_start(s)
        gather_middle(s, T // STRIP, lambda i: i + rim)
        return made

    for s in range(2):
        object_in[s].wait()
        for c in range(2):
            first, last = swap(obj_ref[s, c, :, 0:N]), swap(obj_ref[s, c, :, N : 2 * N])
            ext[s][c, 0, own, :] = first
            ext[s][c, 1, own, :] = pick(first, last)
            ext[s][c, 2, own, :] = last
        halo_pack(s)
    lax.fori_loop(0, SLOTS, prepare, 0)
    probe_in.wait()
    tab_in.wait()
    amps_in.wait()
    pl.semaphore_wait(barrier, 8)
    halos = [halo_start(s) for s in range(2)]

    for iteration in range(ITERS):
        last = iteration == ITERS - 1
        halo_end(0, halos[0])
        loop(ahead)
        halo_end(1, halos[1])
        loop(detect)
        if last:
            one = exchange(1)
            loop(behind)
            zero = exchange(0)
        else:
            loop(behind)
            zero = exchange(0)
            one = exchange(1)
        stores = []
        for s, copies in ((1, one), (0, zero)) if last else ((0, zero), (1, one)):
            grad_end(s, copies, last)
            if last:
                stores.append(load(out_ref.at[s], out_hbm.at[s], 5 + s))
            else:
                halo_pack(s)
                halos[s] = halo_start(s)
    for made in stores:
        made.wait()


COPIES = 64


def solution(mesh):
    rows_n, cols_n = mesh.shape["row"], mesh.shape["col"]
    hbm = pl.BlockSpec(memory_space=pl.ANY)
    smem = pl.BlockSpec(memory_space=pltpu.SMEM)

    def body(object_slices, probe, amplitudes, scan_pos, scan_count):
        tab = jnp.asarray(tables())
        call = pl.pallas_call(
            functools.partial(kernel, rows_n, cols_n),
            out_shape=jax.ShapeDtypeStruct(object_slices.shape, F32),
            in_specs=[smem, smem, hbm, hbm, hbm, hbm],
            out_specs=hbm,
            scratch_shapes=[
                pltpu.VMEM((2, 2, T, T), F32),
                pltpu.VMEM((2, N, N), F32),
                pltpu.VMEM((SLOTS, N, N), F32),
                pltpu.VMEM((8, 2 * N, 2 * N), BF16),
                pltpu.VMEM((2, 2, T, T), F32),
                pltpu.VMEM((2, LANES, E, N), F32),
                pltpu.VMEM((2, LANES, E, N), F32),
                pltpu.VMEM((2, LANES, E, N), F32),
                pltpu.VMEM((2, LANES, E, N), F32),
                pltpu.VMEM((SLOTS, 2, N, N), F32),
                pltpu.VMEM((SLOTS, 2, N, N), F32),
                pltpu.VMEM((SLOTS, 2, 2, GROWS, N), F32),
                pltpu.VMEM((SLOTS, 2, 2, GROWS, N), F32),
                pltpu.VMEM((SLOTS, 3, 8, N), F32),
                pltpu.VMEM((2, 2, T, N), F32),
                pltpu.VMEM((2, 2, E, N), F32),
                pltpu.VMEM((2, 2, E, N), F32),
                pltpu.VMEM((2, 2, E, N), F32),
                pltpu.VMEM((2, 2, LANES, HALF, N), F32),
                pltpu.VMEM((2, 2, LANES, HALF, N), F32),
                pltpu.SemaphoreType.DMA((COPIES,)),
                pltpu.SemaphoreType.DMA((COPIES,)),
                pltpu.SemaphoreType.DMA((7,)),
            ],
            compiler_params=pltpu.CompilerParams(
                collective_id=0, has_side_effects=True, vmem_limit_bytes=56 * 2**20
            ),
        )
        return call(
            scan_pos.reshape(2, SLOTS), scan_count, object_slices, probe,
            amplitudes.reshape(SLOTS, N, N), tab,
        )

    in_specs = (
        P(None, None, "row", "col"),
        P(),
        P("row", "col", None, None, None),
        P(None, "row", "col", None),
        P("row", "col"),
    )
    out_specs = P(None, None, "row", "col")
    return jax.shard_map(body, mesh=mesh, in_specs=in_specs, out_specs=out_specs, check_vma=False)
```

```python
import functools
import math

import jax
import jax.numpy as jnp
import numpy as np
from jax import lax
from jax.experimental import pallas as pl
from jax.experimental.pallas import tpu as pltpu
from jax.sharding import PartitionSpec as P

ITERS = 2
MESH = pl.DeviceIdType.MESH
F32 = jnp.float32
BF16 = jnp.bfloat16

modulus_offset = 0.5
fresnel_scale = 0.9

N = 128
T = 256
E = T + N
HALF = N // 2
LANES = E // N
SLOTS = 16
GROUP = 4
STRIP = 64
SHIFTED = N + 8
GROWS = SHIFTED + 2 * STRIP


def tables():
    positions = np.arange(N)
    frequency = np.where(positions < N // 2, positions, positions - N).astype(np.float64)
    angle = -2.0 * math.pi / N * (np.outer(positions, positions) % N)
    dft = (np.cos(angle) + 1j * np.sin(angle)) / math.sqrt(N)
    phase = math.pi * fresnel_scale * frequency**2 / N
    spread = np.conj(dft) @ (np.exp(1j * phase)[:, None] * dft)
    spread = 0.5 * (spread + spread.T)
    made = []
    for matrix in (spread, dft):
        left = np.block([[matrix.real, -matrix.imag], [matrix.imag, matrix.real]])
        for form in (left, left.T):
            high = form.astype(np.float32).astype(BF16)
            low = (form - high.astype(np.float64)).astype(np.float32).astype(BF16)
            made += [high, low]
    return np.stack(made)


def split(value):
    high = value.astype(BF16)
    return high, (value - high.astype(F32)).astype(BF16)


def dot(a, b):
    return jnp.dot(a, b, preferred_element_type=F32)


def kernel(
    rows_n, cols_n,
    pos_ref, count_ref, obj_hbm, probe_hbm, amps_hbm, tab_hbm,
    out_hbm,
    obj_ref, probe_ref, amps_ref, tab_ref, out_ref,
    ext0, ext1, acc0, acc1, inc_ref, lay_ref, grad0, grad1, mask_ref,
    halo_src, halo_dst, fin_src, fin_dst, up_ref, down_ref,
    send_sem, recv_sem, local_sem,
):
    row, col = lax.axis_index("row"), lax.axis_index("col")
    above, below = lax.rem(row + rows_n - 1, rows_n), lax.rem(row + 1, rows_n)
    before, behind_col = lax.rem(col + cols_n - 1, cols_n), lax.rem(col + 1, cols_n)
    up, down, left, right = (above, col), (below, col), (row, before), (row, behind_col)
    corners = (((above, before), (below, before)), ((above, behind_col), (below, behind_col)))
    has_up, has_down = row > 0, row < rows_n - 1
    has_left, has_right = col > 0, col < cols_n - 1
    ext, acc, grads = (ext0, ext1), (acc0, acc1), (grad0, grad1)
    used = [0]

    barrier = pltpu.get_barrier_semaphore()
    for device in (*corners[0], *corners[1], left, right, up, down):
        pl.semaphore_signal(barrier, inc=1, device_id=device, device_id_type=MESH)

    def load(source, target, index):
        made = pltpu.make_async_copy(source, target, local_sem.at[index])
        made.start()
        return made

    object_in = [load(obj_hbm.at[s], obj_ref.at[s], s) for s in range(2)]
    probe_in = load(probe_hbm, probe_ref, 2)
    tab_in = load(tab_hbm, tab_ref, 3)
    amps_in = load(amps_hbm, amps_ref, 4)

    def copy(source, target, device):
        index = used[0]
        used[0] += 1
        made = pltpu.make_async_remote_copy(
            src_ref=source, dst_ref=target, send_sem=send_sem.at[index],
            recv_sem=recv_sem.at[index], device_id=device, device_id_type=MESH,
        )
        made.start()
        return made

    def wait(copies):
        for made in copies:
            made.wait()

    lane = lax.broadcasted_iota(jnp.int32, (N, N), 1)

    def swap(value):
        return pltpu.roll(value, HALF, 1)

    def lows(value):
        return lax.broadcasted_iota(jnp.int32, value.shape, 1) < HALF

    def pick(in_low, in_high):
        return jnp.where(lows(in_low), in_low, in_high)

    def place(k):
        at_row, at_col = pos_ref[0, k], pos_ref[1, k]
        return (at_row >> 3) & (T // 8 - 1), at_row & 7, (at_col >> 7) & 1, at_col & (N - 1)

    def prepare(k, carry):
        _, _, at_lane, shift = place(k)
        live = (k < count_ref[0, 0]).astype(F32)
        upper = (lax.broadcasted_iota(jnp.int32, (8, N), 1) >= shift).astype(F32)
        mask_ref[k, 0] = upper * live
        mask_ref[k, 1] = (1.0 - upper) * live
        mask_ref[k, 2] = jnp.zeros((8, N), F32) + (1 - at_lane).astype(F32)
        for c in range(2):
            for half in range(2):
                for grad in grads:
                    grad[k, c, half, 0:STRIP, :] = jnp.zeros((STRIP, N), F32)
                    grad[k, c, half, GROWS - STRIP : GROWS, :] = jnp.zeros((STRIP, N), F32)
        return carry

    own, head, tail = slice(HALF, HALF + T), slice(0, HALF), slice(HALF + T, E)

    def edges(source, target, s):
        made = []
        begin = source.shape[2] - T
        first, last, whole = slice(0, HALF), slice(source.shape[2] - HALF, source.shape[2]), slice(begin // 2, begin // 2 + T)
        for side in range(2):
            made.append(copy(source.at[s, side, first], target.at[s, 1 - side, tail], corners[side][0]))
            made.append(copy(source.at[s, side, last], target.at[s, 1 - side, head], corners[side][1]))
        for side, device in enumerate((left, right)):
            made.append(copy(source.at[s, side, whole], target.at[s, 1 - side, own], device))
        return made

    def halo_pack(s):
        halo_src[s, 0] = pick(swap(ext[s][1, 0, own, :]), ext[s][0, 0, own, :])
        halo_src[s, 1] = pick(ext[s][0, 2, own, :], swap(ext[s][1, 2, own, :]))

    def halo_start(s):
        return edges(halo_src, halo_dst, s) + [
            copy(ext[s].at[:, :, HALF : 2 * HALF, :], ext[s].at[:, :, tail, :], up),
            copy(ext[s].at[:, :, T : T + HALF, :], ext[s].at[:, :, head, :], down),
        ]

    def halo_end(s, copies):
        wait(copies)
        for part, inside in ((head, has_up), (own, None), (tail, has_down)):
            for t in range(LANES):
                if t == 1 and inside is None:
                    continue
                for c in range(2):
                    value = ext[s][c, t, part, :]
                    if t != 1:
                        strip = jnp.where((has_left, None, has_right)[t], halo_dst[s, t // 2, part, :], 0.0)
                        strip = strip if c == 0 else swap(strip)
                        value = pick(strip, value) if t == 0 else pick(value, strip)
                    ext[s][c, t, part, :] = value if inside is None else jnp.where(inside, value, 0.0)

    def grad_start(s):
        fin_src[s, 0] = pick(acc[s][0, 0], swap(acc[s][1, 0]))
        fin_src[s, 1] = pick(swap(acc[s][1, 2]), acc[s][0, 2])
        made = edges(fin_src, fin_dst, s)
        rim = HALF // STRIP
        gather_middle(s, 2 * rim, lambda i: i + (i // rim) * (T // STRIP))
        return made + [
            copy(acc[s].at[:, :, head, :], down_ref.at[s], up),
            copy(acc[s].at[:, :, tail, :], up_ref.at[s], down),
        ]

    def grad_end(s, copies, last):
        wait(copies)
        for p in range(T // HALF):
            part = slice(HALF * (p + 1), HALF * (p + 2))
            strips = []
            for side, there in enumerate((has_left, has_right)):
                strip = fin_dst[s, side, part, :]
                if p == 0:
                    strip = strip + jnp.where(has_up, fin_dst[s, side, head, :], 0.0)
                if p == T // HALF - 1:
                    strip = strip + jnp.where(has_down, fin_dst[s, side, tail, :], 0.0)
                strips.append(jnp.where(there, strip, 0.0))
            for c in range(2):
                made = []
                for t in range(LANES):
                    value = ext[s][c, t, part, :] - acc[s][c, t, part, :]
                    if t != 1:
                        value = value - (strips[t // 2] if c == 0 else swap(strips[t // 2]))
                    if p == 0:
                        value = value - jnp.where(has_up, up_ref[s, c, t], 0.0)
                    if p == T // HALF - 1:
                        value = value - jnp.where(has_down, down_ref[s, c, t], 0.0)
                    made.append(value)
                if last:
                    made = [swap(value) for value in made]
                    out_ref[s, c, HALF * p : HALF * (p + 1), 0:N] = pick(made[0], made[1])
                    out_ref[s, c, HALF * p : HALF * (p + 1), N : 2 * N] = pick(made[1], made[2])
                else:
                    for t in range(LANES):
                        ext[s][c, t, part, :] = made[t]

    def patch(s, k):
        eighth, over, at_lane, shift = place(k)
        rows = pl.ds(eighth * 8, SHIFTED)
        parts = []
        for c in range(2):
            here, after = ext[s][c, at_lane, rows, :], ext[s][c, at_lane + 1, rows, :]
            both = jnp.where(lax.broadcasted_iota(jnp.int32, (SHIFTED, N), 1) >= shift, here, after)
            both = pltpu.roll(both, 8 - over, 0)[SHIFTED - N :]
            parts.append(pltpu.roll(both, (N - shift) & (N - 1), 1))
        return parts

    def put(s, k, parts):
        _, over, _, shift = place(k)
        for c in range(2):
            moved = tall([pltpu.roll(parts[c], shift, 1), jnp.zeros((SHIFTED - N, N), F32)])
            moved = pltpu.roll(moved, over, 0)
            for half in range(2):
                grads[s][k, c, half, STRIP : STRIP + SHIFTED, :] = moved * tall([mask_ref[k, half]] * (SHIFTED // 8))

    def tall(parts):
        return jnp.concatenate(parts, axis=0)

    def wide(parts):
        return jnp.concatenate(parts, axis=1)

    def apply(which, waves):
        high_l, low_l = tab_ref[2 * which], tab_ref[2 * which + 1]
        other = which ^ 1
        high_r, low_r = tab_ref[2 * other], tab_ref[2 * other + 1]
        high, low_part = split(tall([wide([wave[c] for wave in waves]) for c in range(2)]))
        mid = dot(wide([high_l, high_l, low_l]), tall([high, low_part, high]))
        high, low_part = split(
            tall([wide([mid[:N, i * N : i * N + N], mid[N:, i * N : i * N + N]]) for i in range(len(waves))])
        )
        done = dot(wide([high, low_part, high]), tall([high_r, high_r, low_r]))
        return [(done[i * N : i * N + N, :N], done[i * N : i * N + N, N:]) for i in range(len(waves))]

    def product(a, b):
        return a[0] * b[0] - a[1] * b[1], a[0] * b[1] + a[1] * b[0]

    def product_conj(a, b):
        return a[0] * b[0] + a[1] * b[1], a[0] * b[1] - a[1] * b[0]

    SPREAD, SPREAD_ADJ, DFT, DFT_INV = 0, 1, 2, 3

    def loop(stage):
        for start in range(0, SLOTS, GROUP):
            stage(range(start, start + GROUP))

    def ahead(slots):
        illum = (probe_ref[0], probe_ref[1])
        waves = apply(SPREAD, [product(illum, patch(0, k)) for k in slots])
        for k, wave in zip(slots, waves):
            inc_ref[k, 0], inc_ref[k, 1] = wave

    def detect(slots):
        exits = []
        for k in slots:
            layer = patch(1, k)
            lay_ref[k, 0], lay_ref[k, 1] = layer
            exits.append(product((inc_ref[k, 0], inc_ref[k, 1]), layer))
        residuals = []
        for k, (re, im) in zip(slots, apply(DFT, exits)):
            factor = 1.0 - amps_ref[k] * lax.rsqrt(re * re + im * im + modulus_offset)
            residuals.append((re * factor, im * factor))
        for k, back in zip(slots, apply(DFT_INV, residuals)):
            put(1, k, product_conj((inc_ref[k, 0], inc_ref[k, 1]), back))
            lay_ref[k, 0], lay_ref[k, 1] = product_conj((lay_ref[k, 0], lay_ref[k, 1]), back)

    def behind(slots):
        illum = (probe_ref[0], probe_ref[1])
        for k, back in zip(slots, apply(SPREAD_ADJ, [(lay_ref[k, 0], lay_ref[k, 1]) for k in slots])):
            put(0, k, product_conj(illum, back))

    def strips_of(s, k, half, at):
        from_row = jnp.clip(at - place(k)[0] + STRIP // 8, 0, (GROWS - STRIP) // 8) * 8
        return [grads[s][k, c, half, pl.ds(from_row, STRIP), :] for c in range(2)]

    def gather_sides(s):
        def step(block, carry):
            at = block * STRIP
            both = [jnp.zeros((STRIP, N), F32)] * 2
            first = [jnp.zeros((STRIP, N), F32)] * 2
            for k in range(SLOTS):
                keep = tall([mask_ref[k, 2]] * (STRIP // 8))
                for c, part in enumerate(strips_of(s, k, place(k)[2], block * (STRIP // 8))):
                    both[c] = both[c] + part
                    first[c] = first[c] + part * keep
            for c in range(2):
                acc[s][c, 0, pl.ds(pl.multiple_of(at, STRIP), STRIP), :] = first[c]
                acc[s][c, 2, pl.ds(pl.multiple_of(at, STRIP), STRIP), :] = both[c] - first[c]
            return carry

        lax.fori_loop(0, E // STRIP, step, 0)

    def gather_middle(s, number, strip_at):
        def step(block, carry):
            at = strip_at(block) * STRIP
            total = [jnp.zeros((STRIP, N), F32)] * 2
            for k in range(SLOTS):
                for c, part in enumerate(strips_of(s, k, 1 - place(k)[2], strip_at(block) * (STRIP // 8))):
                    total[c] = total[c] + part
            for c in range(2):
                acc[s][c, 1, pl.ds(pl.multiple_of(at, STRIP), STRIP), :] = total[c]
            return carry

        lax.fori_loop(0, number, step, 0)

    def exchange(s):
        gather_sides(s)
        made = grad_start(s)
        gather_middle(s, T // STRIP, lambda i: i + HALF // STRIP)
        return made

    for s in range(2):
        object_in[s].wait()
        for c in range(2):
            first, last = swap(obj_ref[s, c, :, 0:N]), swap(obj_ref[s, c, :, N : 2 * N])
            ext[s][c, 0, own, :] = first
            ext[s][c, 1, own, :] = pick(first, last)
            ext[s][c, 2, own, :] = last
        halo_pack(s)
    lax.fori_loop(0, SLOTS, prepare, 0)
    probe_in.wait()
    tab_in.wait()
    amps_in.wait()
    pl.semaphore_wait(barrier, 8)
    halos = [halo_start(s) for s in range(2)]

    for iteration in range(ITERS):
        last = iteration == ITERS - 1
        halo_end(0, halos[0])
        loop(ahead)
        halo_end(1, halos[1])
        loop(detect)
        if last:
            one = exchange(1)
            loop(behind)
            zero = exchange(0)
        else:
            loop(behind)
            zero = exchange(0)
            one = exchange(1)
        stores = []
        for s, copies in ((1, one), (0, zero)) if last else ((0, zero), (1, one)):
            grad_end(s, copies, last)
            if last:
                stores.append(load(out_ref.at[s], out_hbm.at[s], 5 + s))
            else:
                halo_pack(s)
                halos[s] = halo_start(s)
    for made in stores:
        made.wait()


COPIES = 64


def solution(mesh):
    rows_n, cols_n = mesh.shape["row"], mesh.shape["col"]
    hbm = pl.BlockSpec(memory_space=pl.ANY)
    smem = pl.BlockSpec(memory_space=pltpu.SMEM)

    def body(object_slices, probe, amplitudes, scan_pos, scan_count):
        tab = jnp.asarray(tables())
        call = pl.pallas_call(
            functools.partial(kernel, rows_n, cols_n),
            out_shape=jax.ShapeDtypeStruct(object_slices.shape, F32),
            in_specs=[smem, smem, hbm, hbm, hbm, hbm],
            out_specs=hbm,
            scratch_shapes=[
                pltpu.VMEM((2, 2, T, T), F32),
                pltpu.VMEM((2, N, N), F32),
                pltpu.VMEM((SLOTS, N, N), F32),
                pltpu.VMEM((8, 2 * N, 2 * N), BF16),
                pltpu.VMEM((2, 2, T, T), F32),
                pltpu.VMEM((2, LANES, E, N), F32),
                pltpu.VMEM((2, LANES, E, N), F32),
                pltpu.VMEM((2, LANES, E, N), F32),
                pltpu.VMEM((2, LANES, E, N), F32),
                pltpu.VMEM((SLOTS, 2, N, N), F32),
                pltpu.VMEM((SLOTS, 2, N, N), F32),
                pltpu.VMEM((SLOTS, 2, 2, GROWS, N), F32),
                pltpu.VMEM((SLOTS, 2, 2, GROWS, N), F32),
                pltpu.VMEM((SLOTS, 3, 8, N), F32),
                pltpu.VMEM((2, 2, T, N), F32),
                pltpu.VMEM((2, 2, E, N), F32),
                pltpu.VMEM((2, 2, E, N), F32),
                pltpu.VMEM((2, 2, E, N), F32),
                pltpu.VMEM((2, 2, LANES, HALF, N), F32),
                pltpu.VMEM((2, 2, LANES, HALF, N), F32),
                pltpu.SemaphoreType.DMA((COPIES,)),
                pltpu.SemaphoreType.DMA((COPIES,)),
                pltpu.SemaphoreType.DMA((7,)),
            ],
            compiler_params=pltpu.CompilerParams(
                collective_id=0, has_side_effects=True, vmem_limit_bytes=56 * 2**20
            ),
        )
        return call(
            scan_pos.reshape(2, SLOTS), scan_count, object_slices, probe,
            amplitudes.reshape(SLOTS, N, N), tab,
        )

    in_specs = (
        P(None, None, "row", "col"),
        P(),
        P("row", "col", None, None, None),
        P(None, "row", "col", None),
        P("row", "col"),
    )
    out_specs = P(None, None, "row", "col")
    return jax.shard_map(body, mesh=mesh, in_specs=in_specs, out_specs=out_specs, check_vma=False)
```
